512 devices in a mesh: row: 16 (over y_hi, x), col: 32 (over z, y_lo, core).
Axes of the slice: x: 4, y: 8 (y_hi: 4, y_lo: 2; y = y_hi * 2 + y_lo), z: 8, core: 2. Of those that a mesh axis runs over, the one named last changes fastest.
Arguments:
- panel_factor: bfloat16 [128, 20480], P('row', 'col'), may hold values from -0.5 to 0.5
- diag_inverse: bfloat16 [128, 128], P('col'), may hold values from -0.5 to 0.5
- panel_rhs: bfloat16 [128, 18432], P('col', 'row'), may hold values from -6 to 6
- trail_rhs: bfloat16 [18432, 20480], P('row', 'col'), may hold values from -6 to 6
- forward_field: bfloat16 [18432, 20480], P('row', 'col'), may hold values from -6 to 6
- pivot: int32 [128], replicated, may hold values from 0 to 127, each once
- panel_harmonic: int32 [2, 128], replicated, may hold values from 0 to 90
- trail_harmonic: int32 [2, 20480], P(None, 'col'), may hold values from 0 to 90
Outputs:
- panel_adjoint: bfloat16 [128, 18432], P(None, 'row')
- trail_update: bfloat16 [18432, 20480], P('row', 'col')
- eps_grad: float32 [36864], P(('row', 'col'))
The draws below stay inside these ranges and needn't reach their ends.
All inputs are finite; a program needn't handle non-finite values.
Results may differ from the reference program's by a relative error of at most 0.0039.
Values may be sent and summed in bfloat16 or wider, within the bound.
A program may use at most 64 MiB of HBM per device.

```python
import math
import jax
import jax.numpy as jnp
from jax import lax

NB = 128
NT = 20480
S = 18432
ORDERS = 91
DPITCH = 192
NDIAG = 36864


def set_ends(result, rng, least, largest):
    index_at = [jax.random.randint(jax.random.fold_in(rng, axis), (), 0, length) for axis, length in enumerate(result.shape)]
    longest = result.shape.index(max(result.shape))
    next_to = index_at[:longest] + [(index_at[longest] + 1) % result.shape[longest]] + index_at[longest + 1:]
    return result.at[tuple(index_at)].set(least).at[tuple(next_to)].set(largest)


def shard_levels(rng, extent, shards, least, largest):
    def one(axis_at, shards_of):
        draws = jax.random.uniform(jax.random.fold_in(jax.random.fold_in(rng, 6), axis_at), (shards_of,), jnp.float32, least / len(shards), largest / len(shards))
        return jnp.repeat(jnp.exp(draws), extent[axis_at] // shards_of).reshape((-1,) + (1,) * (len(extent) - axis_at - 1))

    factor_of = one(*shards[0])
    for cut in shards[1:]:
        factor_of = factor_of * one(*cut)
    return factor_of


def centred(rng, dims, deviation, most, split=(), kind=jnp.bfloat16):
    entries = jax.random.normal(rng, dims, jnp.float32) * deviation
    if len(split) > 0:
        entries = shard_levels(rng, dims, split, -0.22, 0.18) * entries
    return jnp.clip(entries, min=-most, max=most).astype(kind)


def setup_inputs(seed: int = 0) -> dict:
    keys = jax.random.split(jax.random.key(seed), 9)
    panel_factor = centred(keys[0], (NB, NT), NB ** -0.5, 0.5, ((0, 16), (1, 32)))
    diag_inverse = centred(keys[1], (NB, NB), NB ** -0.5, 0.5, ((0, 32),))
    panel_rhs = centred(keys[2], (NB, S), 1.0, 6.0, ((0, 32), (1, 16)))
    trail_rhs = centred(keys[3], (S, NT), 1.0, 6.0, ((0, 16), (1, 32)))
    forward_field = centred(keys[4], (S, NT), 1.0, 6.0, ((0, 16), (1, 32)))
    pivot = jax.random.permutation(keys[5], NB).astype(jnp.int32)
    panel_harmonic = set_ends(jax.random.randint(keys[6], (2, NB), 0, ORDERS), jax.random.fold_in(keys[6], 1), 0, ORDERS - 1).astype(jnp.int32)
    trail_harmonic = set_ends(jax.random.randint(keys[7], (2, NT), 0, ORDERS), jax.random.fold_in(keys[7], 1), 0, ORDERS - 1).astype(jnp.int32)
    return dict(panel_factor=panel_factor, diag_inverse=diag_inverse, panel_rhs=panel_rhs, trail_rhs=trail_rhs, forward_field=forward_field, pivot=pivot, panel_harmonic=panel_harmonic, trail_harmonic=trail_harmonic)


def reference(panel_factor, diag_inverse, panel_rhs, trail_rhs, forward_field, pivot, panel_harmonic, trail_harmonic):
    panel_adjoint = jnp.dot(diag_inverse.T, panel_rhs, preferred_element_type=jnp.float32).astype(jnp.bfloat16)
    blocks = 16
    block_size = S // blocks
    trail_blocks = trail_rhs.reshape(blocks, block_size, NT)
    field_blocks = forward_field.reshape(blocks, block_size, NT)
    adjoint_blocks = panel_adjoint.reshape(NB, blocks, block_size).transpose(1, 0, 2)

    def accumulate(correlation, inputs):
        adjoint_piece, trail_piece, field_piece = inputs
        update = jnp.dot(adjoint_piece.T, panel_factor, preferred_element_type=jnp.float32)
        fresh = (trail_piece.astype(jnp.float32) - update).astype(jnp.bfloat16)
        correlation = correlation + jnp.dot(adjoint_piece, field_piece, preferred_element_type=jnp.float32)
        return (correlation, fresh)
    initial = jnp.zeros((NB, NT), jnp.float32)
    correlation, fresh_blocks = lax.scan(accumulate, initial, (adjoint_blocks, trail_blocks, field_blocks))
    trail_update = fresh_blocks.reshape(S, NT)
    harmonic_rows = panel_harmonic[:, pivot]
    delta_x = harmonic_rows[0][:, None] - trail_harmonic[0][None, :] + (ORDERS - 1)
    delta_y = harmonic_rows[1][:, None] - trail_harmonic[1][None, :] + (ORDERS - 1)
    cell_index = (delta_x * DPITCH + delta_y).astype(jnp.int32).reshape(-1)
    gradient = jax.ops.segment_sum(correlation.reshape(-1), cell_index, num_segments=NDIAG)
    eps_grad = gradient * jnp.float32(1.0 / math.sqrt(S * NB))
    return (panel_adjoint, trail_update, eps_grad)
```

```python
import functools
import math

import jax
import jax.numpy as jnp
from jax import lax
from jax.experimental import pallas as pl
from jax.experimental.pallas import tpu as pltpu
from jax.sharding import PartitionSpec as P

NB = 128
S = 18432
NR = 16
NC = 32
SB = 1152
QB = 640
HALF = 640
MESH = pl.DeviceIdType.MESH
BF = jnp.bfloat16
F32 = jnp.float32


def kernel(
    pf_hbm, dinv_hbm, rhs_hbm, trail_hbm, ff_hbm, piv_hbm, ph_hbm, th_hbm,
    pa_out, tu_out, eps_out,
    pf_v, raw, trail_v, ff_v, th_v, piv_s, ph_s,
    stage, a_land, b_land, pa, corr, c_send, c_land, hot, u_x, g_send, d_land, h_lo, h_hi, e_send, e_land,
    loc, sems,
):
    row = lax.axis_index("row")
    col = lax.axis_index("col")
    core = col % 2

    def row_peer(k):
        return (row + k) % NR

    def col_peer(k):
        return (col + k) % NC

    copies = [
        pltpu.make_async_copy(rhs_hbm, raw.at[:, pl.ds(0, SB)], loc.at[0]),
        pltpu.make_async_copy(dinv_hbm, raw.at[:, pl.ds(SB, NB)], loc.at[1]),
        pltpu.make_async_copy(pf_hbm, pf_v, loc.at[2]),
        pltpu.make_async_copy(th_hbm, th_v, loc.at[3]),
        pltpu.make_async_copy(piv_hbm, piv_s, loc.at[4]),
        pltpu.make_async_copy(ph_hbm, ph_s, loc.at[5]),
        pltpu.make_async_copy(ff_hbm, ff_v, loc.at[6]),
        pltpu.make_async_copy(trail_hbm, trail_v, loc.at[7]),
    ]
    for c in copies:
        c.start()

    barrier = pltpu.get_barrier_semaphore()

    @pl.loop(1, NC)
    def _(k):
        pl.semaphore_signal(barrier, inc=1, device_id=(row, col_peer(k)), device_id_type=MESH)

    @pl.loop(1, NR)
    def _(k):
        pl.semaphore_signal(barrier, inc=1, device_id=(row_peer(k), col), device_id_type=MESH)

    copies[0].wait()
    copies[1].wait()
    stage[0, :, pl.ds(0, HALF)] = raw[:, pl.ds(0, HALF)]
    stage[1, :, pl.ds(0, HALF)] = raw[:, pl.ds(SB - HALF, HALF)]
    for h in range(2):
        stage[h, :, pl.ds(HALF, NB)] = raw[:, pl.ds(SB, NB)]
    copies[2].wait()

    pl.semaphore_wait(barrier, NC - 1 + NR - 1)

    def col_copy(src, dst, target, k):
        return pltpu.make_async_remote_copy(
            src_ref=src, dst_ref=dst, send_sem=sems.at[2 * k], recv_sem=sems.at[2 * k + 1],
            device_id=(row, target), device_id_type=MESH,
        )

    def row_copy(src, dst, target, k):
        return pltpu.make_async_remote_copy(
            src_ref=src, dst_ref=dst, send_sem=sems.at[2 * k], recv_sem=sems.at[2 * k + 1],
            device_id=(target, col), device_id_type=MESH,
        )

    @pl.loop(1, NC)
    def _(k):
        target = col_peer(k)
        col_copy(stage.at[target % 2], a_land.at[col], target, 0).start()

    @pl.loop(1, NR)
    def _(k):
        row_copy(pf_v, b_land.at[row], row_peer(k), 1).start()

    a_land[col] = stage[core]
    b_land[row] = pf_v[...]
    c_land[row] = jnp.zeros((8, QB), BF)

    for c in copies[3:6]:
        c.wait()
    hx_q = th_v[pl.ds(0, 1), :]
    hy_q = th_v[pl.ds(1, 1), :]
    u_x[...] = (lax.broadcasted_iota(jnp.int32, (192, QB), 0) + hx_q - 90).astype(BF)
    hy_c = jnp.transpose(jnp.broadcast_to(hy_q.astype(F32), (128, QB)))
    hy_c = jnp.concatenate([hy_c, hy_c], axis=1).astype(jnp.int32)
    u_y = (lax.broadcasted_iota(jnp.int32, (QB, 256), 1) + hy_c - 90).astype(BF)
    hx_a = []
    for j in range(8):
        unpivoted = piv_s[row * 8 + j]
        hx_a.append(ph_s[0, unpivoted].astype(F32).astype(BF))
        hy = ph_s[1, unpivoted].astype(F32).astype(BF)
        hot[pl.ds(j * QB, QB), :] = jnp.where(u_y == hy, jnp.ones((), BF), jnp.zeros((), BF))

    col_copy(a_land.at[pl.ds(0, NC - 1)], a_land.at[pl.ds(0, NC - 1)], col_peer(1), 0).wait_recv()
    both = a_land[...].astype(F32).reshape(NB, HALF + NB).astype(BF)
    mine = lax.dot_general(
        both[:, HALF:], both[:, :HALF], (((0,), (0,)), ((), ())), preferred_element_type=F32
    ).astype(BF)
    pa[:, pl.ds(pl.multiple_of(core * (SB - HALF), 128), HALF)] = mine
    part = pa.at[:, pl.ds(pl.multiple_of(core * HALF, 128), SB - HALF)]
    swap = col_copy(part, part, col + 1 - 2 * core, 2)
    swap.start()
    copies[6].wait()
    swap.wait()

    corr[...] = jnp.dot(pa[...], ff_v[...], preferred_element_type=F32)
    c_send[...] = corr[...].reshape(NR, 8, QB).astype(BF)

    @pl.loop(1, NR)
    def _(k):
        target = row_peer(k)
        row_copy(c_send.at[target], c_land.at[row], target, 3).start()

    row_copy(b_land.at[pl.ds(0, NR - 1)], b_land.at[pl.ds(0, NR - 1)], row_peer(1), 1).wait_recv()
    factor = b_land[...].astype(F32).reshape(NB, QB).astype(BF)
    copies[7].wait()
    for t in range(3):
        at = pl.ds(t * 384, 384)
        update = lax.dot_general(
            pa[:, at], factor, (((0,), (0,)), ((), ())), preferred_element_type=F32
        )
        tu_out[at, :] = (trail_v[at, :].astype(F32) - update).astype(BF)
    pa_out[...] = pa[...]

    row_copy(c_land.at[pl.ds(0, NR - 1)], c_land.at[pl.ds(0, NR - 1)], row_peer(1), 3).wait_recv()
    total = corr[pl.ds(pl.multiple_of(row * 8, 8), 8), :]
    for r in range(NR):
        total = total + c_land[r].astype(F32)
    high = total.astype(BF)
    low = (total - high.astype(F32)).astype(BF)
    grid = jnp.zeros((384, 256), F32)
    for s in range(2):
        pieces = []
        for j in range(4 * s, 4 * s + 4):
            at_x = u_x[...] == hx_a[j]
            pieces.append(
                jnp.concatenate(
                    [
                        jnp.where(at_x, high[j : j + 1, :], jnp.zeros((), BF)),
                        jnp.where(at_x, low[j : j + 1, :], jnp.zeros((), BF)),
                    ],
                    axis=0,
                )
            )
        grid = grid + jnp.dot(
            jnp.concatenate(pieces, axis=1), hot[pl.ds(s * 4 * QB, 4 * QB), :], preferred_element_type=F32
        )
    grid = grid[:192] + grid[192:]
    for r in range(NR):
        g_send[r] = grid[12 * r : 12 * r + 12]

    @pl.loop(1, NR)
    def _(k):
        target = row_peer(k)
        row_copy(g_send.at[target], d_land.at[row], target, 4).start()

    d_land[row] = g_send[row]
    row_copy(d_land.at[pl.ds(0, NR - 1)], d_land.at[pl.ds(0, NR - 1)], row_peer(1), 4).wait_recv()
    summed = d_land[0]
    for r in range(1, NR):
        summed = summed + d_land[r]
    h_lo[...] = summed[:, :128]
    h_hi[...] = summed[:, 128:]

    flat = jnp.concatenate(
        [piece for t in range(3) for piece in (h_lo[pl.ds(t, 4, 3), :], h_hi[pl.ds(t, 4, 3), :][:, :64])], axis=1
    )
    for h in range(8):
        piece = jnp.concatenate([flat[:, 72 * h : 72 * h + 72], jnp.zeros((4, 56), F32)], axis=1)
        for g in range(4):
            e_send[8 * g + h] = piece[g : g + 1]

    @pl.loop(1, NC)
    def _(k):
        target = col_peer(k)
        col_copy(e_send.at[target], e_land.at[col], target, 5).start()

    e_land[col] = e_send[col]
    col_copy(e_land.at[pl.ds(0, NC - 1)], e_land.at[pl.ds(0, NC - 1)], col_peer(1), 5).wait_recv()
    eps_out[...] = jnp.sum(e_land[...], axis=0) * F32(1.0 / math.sqrt(S * NB))

    col_copy(a_land.at[pl.ds(0, NC - 1)], a_land.at[pl.ds(0, NC - 1)], col_peer(1), 0).wait_send()
    row_copy(b_land.at[pl.ds(0, NR - 1)], b_land.at[pl.ds(0, NR - 1)], row_peer(1), 1).wait_send()
    row_copy(c_land.at[pl.ds(0, NR - 1)], c_land.at[pl.ds(0, NR - 1)], row_peer(1), 3).wait_send()
    row_copy(d_land.at[pl.ds(0, NR - 1)], d_land.at[pl.ds(0, NR - 1)], row_peer(1), 4).wait_send()
    col_copy(e_land.at[pl.ds(0, NC - 1)], e_land.at[pl.ds(0, NC - 1)], col_peer(1), 5).wait_send()


def per_device(*args):
    anywhere = pl.BlockSpec(memory_space=pl.ANY)
    vmem = pl.BlockSpec(memory_space=pltpu.VMEM)
    pa, tu, eps = pl.pallas_call(
        kernel,
        out_shape=(
            jax.ShapeDtypeStruct((NB, SB), BF),
            jax.ShapeDtypeStruct((SB, QB), BF),
            jax.ShapeDtypeStruct((1, 128), F32),
        ),
        in_specs=[anywhere] * 8,
        out_specs=(vmem, vmem, vmem),
        scratch_shapes=[
            pltpu.VMEM((8, QB), BF),
            pltpu.VMEM((4, SB + NB), BF),
            pltpu.VMEM((SB, QB), BF),
            pltpu.VMEM((SB, QB), BF),
            pltpu.VMEM((2, QB), jnp.int32),
            pltpu.SMEM((NB,), jnp.int32),
            pltpu.SMEM((2, NB), jnp.int32),
            pltpu.VMEM((2, 4, HALF + NB), BF),
            pltpu.VMEM((NC, 4, HALF + NB), BF),
            pltpu.VMEM((NR, 8, QB), BF),
            pltpu.VMEM((NB, SB), BF),
            pltpu.VMEM((NB, QB), F32),
            pltpu.VMEM((NR, 8, QB), BF),
            pltpu.VMEM((NR, 8, QB), BF),
            pltpu.VMEM((8 * QB, 256), BF),
            pltpu.VMEM((192, QB), BF),
            pltpu.VMEM((NR, 12, 256), F32),
            pltpu.VMEM((NR, 12, 256), F32),
            pltpu.VMEM((12, 128), F32),
            pltpu.VMEM((12, 128), F32),
            pltpu.VMEM((NC, 1, 128), F32),
            pltpu.VMEM((NC, 1, 128), F32),
            pltpu.SemaphoreType.DMA((8,)),
            pltpu.SemaphoreType.DMA((12,)),
        ],
        compiler_params=pltpu.CompilerParams(
            collective_id=0, has_side_effects=True, vmem_limit_bytes=40 * 2**20
        ),
    )(*args)
    return pa, tu, eps[0, :72]


def solution(mesh):
    placed = (
        P("row", "col"),
        P("col", None),
        P("col", "row"),
        P("row", "col"),
        P("row", "col"),
        P(),
        P(),
        P(None, "col"),
    )
    return jax.shard_map(
        per_device,
        mesh=mesh,
        in_specs=placed,
        out_specs=(P(None, "row"), P("row", "col"), P(("row", "col"))),
        check_vma=False,
    )
```

```python
import functools
import math

import jax
import jax.numpy as jnp
from jax import lax
from jax.experimental import pallas as pl
from jax.experimental.pallas import tpu as pltpu
from jax.sharding import PartitionSpec as P

NB = 128
S = 18432
NR = 16
NC = 32
SB = 1152
QB = 640
HALF = 640
MESH = pl.DeviceIdType.MESH
BF = jnp.bfloat16
F32 = jnp.float32


def kernel(
    pf_hbm, dinv_hbm, rhs_hbm, trail_hbm, ff_hbm, piv_hbm, ph_hbm, th_hbm,
    pa_out, tu_out, eps_out,
    pf_v, raw, trail_v, ff_v, th_v, piv_s, ph_s,
    stage, a_land, b_land, pa, corr, c_send, c_land, hot, u_x, g_send, d_land, h_lo, h_hi, e_send, e_land,
    loc, sems,
):
    row = lax.axis_index("row")
    col = lax.axis_index("col")
    core = col % 2

    def row_peer(k):
        return (row + k) % NR

    def col_peer(k):
        return (col + k) % NC

    copies = [
        pltpu.make_async_copy(rhs_hbm, raw.at[:, pl.ds(0, SB)], loc.at[0]),
        pltpu.make_async_copy(dinv_hbm, raw.at[:, pl.ds(SB, NB)], loc.at[1]),
        pltpu.make_async_copy(pf_hbm, pf_v, loc.at[2]),
        pltpu.make_async_copy(th_hbm, th_v, loc.at[3]),
        pltpu.make_async_copy(piv_hbm, piv_s, loc.at[4]),
        pltpu.make_async_copy(ph_hbm, ph_s, loc.at[5]),
        pltpu.make_async_copy(ff_hbm, ff_v, loc.at[6]),
        pltpu.make_async_copy(trail_hbm, trail_v, loc.at[7]),
    ]
    for c in copies:
        c.start()

    barrier = pltpu.get_barrier_semaphore()

    @pl.loop(1, NC)
    def _(k):
        pl.semaphore_signal(barrier, inc=1, device_id=(row, col_peer(k)), device_id_type=MESH)

    @pl.loop(1, NR)
    def _(k):
        pl.semaphore_signal(barrier, inc=1, device_id=(row_peer(k), col), device_id_type=MESH)

    copies[0].wait()
    copies[1].wait()
    stage[0, :, pl.ds(0, HALF)] = raw[:, pl.ds(0, HALF)]
    stage[1, :, pl.ds(0, HALF)] = raw[:, pl.ds(SB - HALF, HALF)]
    for h in range(2):
        stage[h, :, pl.ds(HALF, NB)] = raw[:, pl.ds(SB, NB)]
    copies[2].wait()

    pl.semaphore_wait(barrier, NC - 1 + NR - 1)

    def col_copy(src, dst, target, k):
        return pltpu.make_async_remote_copy(
            src_ref=src, dst_ref=dst, send_sem=sems.at[2 * k], recv_sem=sems.at[2 * k + 1],
            device_id=(row, target), device_id_type=MESH,
        )

    def row_copy(src, dst, target, k):
        return pltpu.make_async_remote_copy(
            src_ref=src, dst_ref=dst, send_sem=sems.at[2 * k], recv_sem=sems.at[2 * k + 1],
            device_id=(target, col), device_id_type=MESH,
        )

    @pl.loop(1, NC)
    def _(k):
        target = col_peer(k)
        col_copy(stage.at[target % 2], a_land.at[col], target, 0).start()

    @pl.loop(1, NR)
    def _(k):
        row_copy(pf_v, b_land.at[row], row_peer(k), 1).start()

    a_land[col] = stage[core]
    b_land[row] = pf_v[...]
    c_land[row] = jnp.zeros((8, QB), BF)

    for c in copies[3:6]:
        c.wait()
    hx_q = th_v[pl.ds(0, 1), :]
    hy_q = th_v[pl.ds(1, 1), :]
    u_x[...] = (lax.broadcasted_iota(jnp.int32, (192, QB), 0) + hx_q - 90).astype(BF)
    hy_c = jnp.transpose(jnp.broadcast_to(hy_q.astype(F32), (128, QB)))
    hy_c = jnp.concatenate([hy_c, hy_c], axis=1).astype(jnp.int32)
    u_y = (lax.broadcasted_iota(jnp.int32, (QB, 256), 1) + hy_c - 90).astype(BF)
    hx_a = []
    for j in range(8):
        unpivoted = piv_s[row * 8 + j]
        hx_a.append(ph_s[0, unpivoted].astype(F32).astype(BF))
        hy = ph_s[1, unpivoted].astype(F32).astype(BF)
        hot[pl.ds(j * QB, QB), :] = jnp.where(u_y == hy, jnp.ones((), BF), jnp.zeros((), BF))

    col_copy(a_land.at[pl.ds(0, NC - 1)], a_land.at[pl.ds(0, NC - 1)], col_peer(1), 0).wait_recv()
    both = a_land[...].astype(F32).reshape(NB, HALF + NB).astype(BF)
    mine = lax.dot_general(
        both[:, HALF:], both[:, :HALF], (((0,), (0,)), ((), ())), preferred_element_type=F32
    ).astype(BF)
    pa[:, pl.ds(pl.multiple_of(core * (SB - HALF), 128), HALF)] = mine
    part = pa.at[:, pl.ds(pl.multiple_of(core * HALF, 128), SB - HALF)]
    swap = col_copy(part, part, col + 1 - 2 * core, 2)
    swap.start()
    copies[6].wait()
    swap.wait()

    corr[...] = jnp.dot(pa[...], ff_v[...], preferred_element_type=F32)
    c_send[...] = corr[...].reshape(NR, 8, QB).astype(BF)

    @pl.loop(1, NR)
    def _(k):
        target = row_peer(k)
        row_copy(c_send.at[target], c_land.at[row], target, 3).start()

    row_copy(b_land.at[pl.ds(0, NR - 1)], b_land.at[pl.ds(0, NR - 1)], row_peer(1), 1).wait_recv()
    factor = b_land[...].astype(F32).reshape(NB, QB).astype(BF)
    copies[7].wait()
    for t in range(3):
        at = pl.ds(t * 384, 384)
        update = lax.dot_general(
            pa[:, at], factor, (((0,), (0,)), ((), ())), preferred_element_type=F32
        )
        tu_out[at, :] = (trail_v[at, :].astype(F32) - update).astype(BF)
    pa_out[...] = pa[...]

    row_copy(c_land.at[pl.ds(0, NR - 1)], c_land.at[pl.ds(0, NR - 1)], row_peer(1), 3).wait_recv()
    total = corr[pl.ds(pl.multiple_of(row * 8, 8), 8), :]
    for r in range(NR):
        total = total + c_land[r].astype(F32)
    high = total.astype(BF)
    low = (total - high.astype(F32)).astype(BF)
    grid = jnp.zeros((384, 256), F32)
    for s in range(2):
        pieces = []
        for j in range(4 * s, 4 * s + 4):
            at_x = u_x[...] == hx_a[j]
            pieces.append(
                jnp.concatenate(
                    [
                        jnp.where(at_x, high[j : j + 1, :], jnp.zeros((), BF)),
                        jnp.where(at_x, low[j : j + 1, :], jnp.zeros((), BF)),
                    ],
                    axis=0,
                )
            )
        grid = grid + jnp.dot(
            jnp.concatenate(pieces, axis=1), hot[pl.ds(s * 4 * QB, 4 * QB), :], preferred_element_type=F32
        )
    grid = grid[:192] + grid[192:]
    for r in range(NR):
        g_send[r] = grid[12 * r : 12 * r + 12]

    @pl.loop(1, NR)
    def _(k):
        target = row_peer(k)
        row_copy(g_send.at[target], d_land.at[row], target, 4).start()

    d_land[row] = g_send[row]
    row_copy(d_land.at[pl.ds(0, NR - 1)], d_land.at[pl.ds(0, NR - 1)], row_peer(1), 4).wait_recv()
    summed = d_land[0]
    for r in range(1, NR):
        summed = summed + d_land[r]
    h_lo[...] = summed[:, :128]
    h_hi[...] = summed[:, 128:]

    flat = jnp.concatenate(
        [piece for t in range(3) for piece in (h_lo[pl.ds(t, 4, 3), :], h_hi[pl.ds(t, 4, 3), :][:, :64])], axis=1
    )
    for h in range(8):
        piece = jnp.concatenate([flat[:, 72 * h : 72 * h + 72], jnp.zeros((4, 56), F32)], axis=1)
        for g in range(4):
            e_send[8 * g + h] = piece[g : g + 1]

    @pl.loop(1, NC)
    def _(k):
        target = col_peer(k)
        col_copy(e_send.at[target], e_land.at[col], target, 5).start()

    e_land[col] = e_send[col]
    col_copy(e_land.at[pl.ds(0, NC - 1)], e_land.at[pl.ds(0, NC - 1)], col_peer(1), 5).wait_recv()
    eps_out[...] = jnp.sum(e_land[...], axis=0) * F32(1.0 / math.sqrt(S * NB))

    col_copy(a_land.at[pl.ds(0, NC - 1)], a_land.at[pl.ds(0, NC - 1)], col_peer(1), 0).wait_send()
    row_copy(b_land.at[pl.ds(0, NR - 1)], b_land.at[pl.ds(0, NR - 1)], row_peer(1), 1).wait_send()
    row_copy(c_land.at[pl.ds(0, NR - 1)], c_land.at[pl.ds(0, NR - 1)], row_peer(1), 3).wait_send()
    row_copy(d_land.at[pl.ds(0, NR - 1)], d_land.at[pl.ds(0, NR - 1)], row_peer(1), 4).wait_send()
    col_copy(e_land.at[pl.ds(0, NC - 1)], e_land.at[pl.ds(0, NC - 1)], col_peer(1), 5).wait_send()


def finish(pa_in, tu_in, eps_in, pa_out, tu_out, eps_out, sems):
    copies = [
        pltpu.make_async_copy(tu_in, tu_out, sems.at[0]),
        pltpu.make_async_copy(pa_in, pa_out, sems.at[1]),
    ]
    for c in copies:
        c.start()
    eps_out[...] = eps_in[0, :72]
    for c in copies:
        c.wait()


def per_device(*args):
    anywhere = pl.BlockSpec(memory_space=pltpu.HBM)
    vmem = pl.BlockSpec(memory_space=pltpu.VMEM)
    args = [pltpu.with_memory_space_constraint(a, pltpu.HBM) for a in args]
    pa, tu, eps = pl.pallas_call(
        kernel,
        out_shape=(
            jax.ShapeDtypeStruct((NB, SB), BF),
            jax.ShapeDtypeStruct((SB, QB), BF),
            jax.ShapeDtypeStruct((1, 128), F32),
        ),
        in_specs=[anywhere] * 8,
        out_specs=(vmem, vmem, vmem),
        scratch_shapes=[
            pltpu.VMEM((8, QB), BF),
            pltpu.VMEM((4, SB + NB), BF),
            pltpu.VMEM((SB, QB), BF),
            pltpu.VMEM((SB, QB), BF),
            pltpu.VMEM((2, QB), jnp.int32),
            pltpu.SMEM((NB,), jnp.int32),
            pltpu.SMEM((2, NB), jnp.int32),
            pltpu.VMEM((2, 4, HALF + NB), BF),
            pltpu.VMEM((NC, 4, HALF + NB), BF),
            pltpu.VMEM((NR, 8, QB), BF),
            pltpu.VMEM((NB, SB), BF),
            pltpu.VMEM((NB, QB), F32),
            pltpu.VMEM((NR, 8, QB), BF),
            pltpu.VMEM((NR, 8, QB), BF),
            pltpu.VMEM((8 * QB, 256), BF),
            pltpu.VMEM((192, QB), BF),
            pltpu.VMEM((NR, 12, 256), F32),
            pltpu.VMEM((NR, 12, 256), F32),
            pltpu.VMEM((12, 128), F32),
            pltpu.VMEM((12, 128), F32),
            pltpu.VMEM((NC, 1, 128), F32),
            pltpu.VMEM((NC, 1, 128), F32),
            pltpu.SemaphoreType.DMA((8,)),
            pltpu.SemaphoreType.DMA((12,)),
        ],
        compiler_params=pltpu.CompilerParams(
            collective_id=0, has_side_effects=True, vmem_limit_bytes=40 * 2**20
        ),
    )(*args)
    return pl.pallas_call(
        finish,
        out_shape=(
            jax.ShapeDtypeStruct((NB, SB), BF),
            jax.ShapeDtypeStruct((SB, QB), BF),
            jax.ShapeDtypeStruct((72,), F32),
        ),
        in_specs=[vmem] * 3,
        out_specs=(anywhere, anywhere, pl.BlockSpec()),
        scratch_shapes=[pltpu.SemaphoreType.DMA((2,))],
        compiler_params=pltpu.CompilerParams(vmem_limit_bytes=2**20),
    )(pa, tu, eps)


def solution(mesh):
    placed = (
        P("row", "col"),
        P("col", None),
        P("col", "row"),
        P("row", "col"),
        P("row", "col"),
        P(),
        P(),
        P(None, "col"),
    )
    return jax.shard_map(
        per_device,
        mesh=mesh,
        in_specs=placed,
        out_specs=(P(None, "row"), P("row", "col"), P(("row", "col"))),
        check_vma=False,
    )
```

```python
import functools
import math

import jax
import jax.numpy as jnp
from jax import lax
from jax.experimental import pallas as pl
from jax.experimental.pallas import tpu as pltpu
from jax.sharding import PartitionSpec as P

NB = 128
S = 18432
NR = 16
NC = 32
SB = 1152
QB = 640
HALF = 640
MESH = pl.DeviceIdType.MESH
BF = jnp.bfloat16
F32 = jnp.float32


def kernel(
    pf_hbm, dinv_hbm, rhs_hbm, trail_hbm, ff_hbm, piv_hbm, ph_hbm, th_hbm,
    pa_out, tu_out, eps_out,
    pf_v, raw, trail_v, ff_v, th_v, piv_s, ph_s,
    stage, a_land, b_land, pa, corr, c_send, c_land, hot, u_x, g_send, d_land, h_lo, h_hi, e_send, e_land,
    loc, sems,
):
    row = lax.axis_index("row")
    col = lax.axis_index("col")
    core = col % 2

    def row_peer(k):
        return (row + k) % NR

    def col_peer(k):
        return (col + k) % NC

    copies = [
        pltpu.make_async_copy(rhs_hbm, raw.at[:, pl.ds(0, SB)], loc.at[0]),
        pltpu.make_async_copy(dinv_hbm, raw.at[:, pl.ds(SB, NB)], loc.at[1]),
        pltpu.make_async_copy(pf_hbm, pf_v, loc.at[2]),
        pltpu.make_async_copy(th_hbm, th_v, loc.at[3]),
        pltpu.make_async_copy(piv_hbm, piv_s, loc.at[4]),
        pltpu.make_async_copy(ph_hbm, ph_s, loc.at[5]),
        pltpu.make_async_copy(ff_hbm, ff_v, loc.at[6]),
        pltpu.make_async_copy(trail_hbm, trail_v, loc.at[7]),
    ]
    for c in copies:
        c.start()

    barrier = pltpu.get_barrier_semaphore()

    @pl.loop(1, NC)
    def _(k):
        pl.semaphore_signal(barrier, inc=1, device_id=(row, col_peer(k)), device_id_type=MESH)

    @pl.loop(1, NR)
    def _(k):
        pl.semaphore_signal(barrier, inc=1, device_id=(row_peer(k), col), device_id_type=MESH)

    copies[0].wait()
    copies[1].wait()
    mine = raw[...].astype(F32)
    inverse = mine[:, SB:]
    for h in range(2):
        at = h * (SB - HALF)
        stage[h] = jnp.concatenate(
            [mine[:, at : at + 384], jnp.concatenate([mine[:, at + 384 : at + HALF], inverse], axis=1)], axis=0
        ).astype(BF)
    copies[2].wait()

    pl.semaphore_wait(barrier, NC - 1 + NR - 1)

    def col_copy(src, dst, target, k):
        return pltpu.make_async_remote_copy(
            src_ref=src, dst_ref=dst, send_sem=sems.at[2 * k], recv_sem=sems.at[2 * k + 1],
            device_id=(row, target), device_id_type=MESH,
        )

    def row_copy(src, dst, target, k):
        return pltpu.make_async_remote_copy(
            src_ref=src, dst_ref=dst, send_sem=sems.at[2 * k], recv_sem=sems.at[2 * k + 1],
            device_id=(target, col), device_id_type=MESH,
        )

    @pl.loop(1, NC)
    def _(k):
        target = col_peer(k)
        col_copy(stage.at[target % 2], a_land.at[col], target, 0).start()

    @pl.loop(1, NR)
    def _(k):
        row_copy(pf_v, b_land.at[row], row_peer(k), 1).start()

    a_land[col] = stage[core]
    b_land[row] = pf_v[...]
    c_land[row] = jnp.zeros((8, QB), BF)

    for c in copies[3:6]:
        c.wait()
    hx_q = th_v[pl.ds(0, 1), :]
    hy_q = th_v[pl.ds(1, 1), :]
    u_x[...] = (lax.broadcasted_iota(jnp.int32, (192, QB), 0) + hx_q - 90).astype(BF)
    hy_c = jnp.transpose(jnp.broadcast_to(hy_q.astype(F32), (128, QB)))
    hy_c = jnp.concatenate([hy_c, hy_c], axis=1).astype(jnp.int32)
    u_y = (lax.broadcasted_iota(jnp.int32, (QB, 256), 1) + hy_c - 90).astype(BF)
    hx_a = []
    for j in range(8):
        unpivoted = piv_s[row * 8 + j]
        hx_a.append(ph_s[0, unpivoted].astype(F32).astype(BF))
        hy = ph_s[1, unpivoted].astype(F32).astype(BF)
        hot[pl.ds(j * QB, QB), :] = jnp.where(u_y == hy, jnp.ones((), BF), jnp.zeros((), BF))

    col_copy(a_land.at[pl.ds(0, NC - 1)], a_land.at[pl.ds(0, NC - 1)], col_peer(1), 0).wait_recv()
    both = a_land[...].astype(F32).reshape(2 * NB, 384)
    odd = lax.broadcasted_iota(jnp.int32, (2 * NB, NB), 0) % 8 >= 4
    inverse = jnp.where(odd, both[:, 256:], 0.0)
    both = both.astype(BF)
    contract = (((0,), (0,)), ((), ()))
    mine = jnp.concatenate(
        [
            lax.dot_general(
                jnp.roll(inverse, -4, axis=0).astype(BF), both, contract, preferred_element_type=F32
            ),
            lax.dot_general(inverse.astype(BF), both[:, :256], contract, preferred_element_type=F32),
        ],
        axis=1,
    ).astype(BF)
    pa[:, pl.ds(pl.multiple_of(core * (SB - HALF), 128), HALF)] = mine
    part = pa.at[:, pl.ds(pl.multiple_of(core * HALF, 128), SB - HALF)]
    swap = col_copy(part, part, col + 1 - 2 * core, 2)
    swap.start()
    copies[6].wait()
    swap.wait()

    corr[...] = jnp.dot(pa[...], ff_v[...], preferred_element_type=F32)
    c_send[...] = corr[...].reshape(NR, 8, QB).astype(BF)

    @pl.loop(1, NR)
    def _(k):
        target = row_peer(k)
        row_copy(c_send.at[target], c_land.at[row], target, 3).start()

    row_copy(b_land.at[pl.ds(0, NR - 1)], b_land.at[pl.ds(0, NR - 1)], row_peer(1), 1).wait_recv()
    factor = b_land[...].astype(F32).reshape(NB, QB).astype(BF)
    copies[7].wait()
    for t in range(3):
        at = pl.ds(t * 384, 384)
        update = lax.dot_general(
            pa[:, at], factor, (((0,), (0,)), ((), ())), preferred_element_type=F32
        )
        tu_out[at, :] = (trail_v[at, :].astype(F32) - update).astype(BF)
    pa_out[...] = pa[...]

    row_copy(c_land.at[pl.ds(0, NR - 1)], c_land.at[pl.ds(0, NR - 1)], row_peer(1), 3).wait_recv()
    total = corr[pl.ds(pl.multiple_of(row * 8, 8), 8), :]
    for r in range(NR):
        total = total + c_land[r].astype(F32)
    high = total.astype(BF)
    low = (total - high.astype(F32)).astype(BF)
    grid = jnp.zeros((384, 256), F32)
    for s in range(2):
        pieces = []
        for j in range(4 * s, 4 * s + 4):
            at_x = u_x[...] == hx_a[j]
            pieces.append(
                jnp.concatenate(
                    [
                        jnp.where(at_x, high[j : j + 1, :], jnp.zeros((), BF)),
                        jnp.where(at_x, low[j : j + 1, :], jnp.zeros((), BF)),
                    ],
                    axis=0,
                )
            )
        grid = grid + jnp.dot(
            jnp.concatenate(pieces, axis=1), hot[pl.ds(s * 4 * QB, 4 * QB), :], preferred_element_type=F32
        )
    grid = grid[:192] + grid[192:]
    for r in range(NR):
        g_send[r] = jnp.concatenate([grid[12 * r : 12 * r + 12], jnp.zeros((4, 256), F32)], axis=0).astype(BF)

    @pl.loop(1, NR)
    def _(k):
        target = row_peer(k)
        row_copy(g_send.at[target], d_land.at[row], target, 4).start()

    d_land[row] = g_send[row]
    row_copy(d_land.at[pl.ds(0, NR - 1)], d_land.at[pl.ds(0, NR - 1)], row_peer(1), 4).wait_recv()
    summed = d_land[0].astype(F32)
    for r in range(1, NR):
        summed = summed + d_land[r].astype(F32)
    h_lo[...] = summed[:, :128]
    h_hi[...] = summed[:, 128:]

    flat = jnp.concatenate(
        [piece for t in range(3) for piece in (h_lo[pl.ds(t, 4, 3), :], h_hi[pl.ds(t, 4, 3), :][:, :64])], axis=1
    )
    for h in range(8):
        piece = jnp.concatenate([flat[:, 72 * h : 72 * h + 72], jnp.zeros((4, 56), F32)], axis=1)
        for g in range(4):
            e_send[8 * g + h] = piece[g : g + 1]

    @pl.loop(1, NC)
    def _(k):
        target = col_peer(k)
        col_copy(e_send.at[target], e_land.at[col], target, 5).start()

    e_land[col] = e_send[col]
    col_copy(e_land.at[pl.ds(0, NC - 1)], e_land.at[pl.ds(0, NC - 1)], col_peer(1), 5).wait_recv()
    eps_out[...] = jnp.sum(e_land[...], axis=0) * F32(1.0 / math.sqrt(S * NB))

    col_copy(a_land.at[pl.ds(0, NC - 1)], a_land.at[pl.ds(0, NC - 1)], col_peer(1), 0).wait_send()
    row_copy(b_land.at[pl.ds(0, NR - 1)], b_land.at[pl.ds(0, NR - 1)], row_peer(1), 1).wait_send()
    row_copy(c_land.at[pl.ds(0, NR - 1)], c_land.at[pl.ds(0, NR - 1)], row_peer(1), 3).wait_send()
    row_copy(d_land.at[pl.ds(0, NR - 1)], d_land.at[pl.ds(0, NR - 1)], row_peer(1), 4).wait_send()
    col_copy(e_land.at[pl.ds(0, NC - 1)], e_land.at[pl.ds(0, NC - 1)], col_peer(1), 5).wait_send()


def finish(pa_in, tu_in, eps_in, pa_out, tu_out, eps_out, sems):
    copies = [
        pltpu.make_async_copy(tu_in.at[pl.ds(k * 288, 288)], tu_out.at[pl.ds(k * 288, 288)], sems.at[k])
        for k in range(4)
    ]
    copies.append(pltpu.make_async_copy(pa_in, pa_out, sems.at[4]))
    for c in copies:
        c.start()
    eps_out[...] = eps_in[0, :72]
    for c in copies:
        c.wait()


def per_device(*args):
    anywhere = pl.BlockSpec(memory_space=pltpu.HBM)
    vmem = pl.BlockSpec(memory_space=pltpu.VMEM)
    args = [pltpu.with_memory_space_constraint(a, pltpu.HBM) for a in args]
    pa, tu, eps = pl.pallas_call(
        kernel,
        out_shape=(
            jax.ShapeDtypeStruct((NB, SB), BF),
            jax.ShapeDtypeStruct((SB, QB), BF),
            jax.ShapeDtypeStruct((1, 128), F32),
        ),
        in_specs=[anywhere] * 8,
        out_specs=(vmem, vmem, vmem),
        scratch_shapes=[
            pltpu.VMEM((8, QB), BF),
            pltpu.VMEM((4, SB + NB), BF),
            pltpu.VMEM((SB, QB), BF),
            pltpu.VMEM((SB, QB), BF),
            pltpu.VMEM((2, QB), jnp.int32),
            pltpu.SMEM((NB,), jnp.int32),
            pltpu.SMEM((2, NB), jnp.int32),
            pltpu.VMEM((2, 8, 384), BF),
            pltpu.VMEM((NC, 8, 384), BF),
            pltpu.VMEM((NR, 8, QB), BF),
            pltpu.VMEM((NB, SB), BF),
            pltpu.VMEM((NB, QB), F32),
            pltpu.VMEM((NR, 8, QB), BF),
            pltpu.VMEM((NR, 8, QB), BF),
            pltpu.VMEM((8 * QB, 256), BF),
            pltpu.VMEM((192, QB), BF),
            pltpu.VMEM((NR, 16, 256), BF),
            pltpu.VMEM((NR, 16, 256), BF),
            pltpu.VMEM((16, 128), F32),
            pltpu.VMEM((16, 128), F32),
            pltpu.VMEM((NC, 1, 128), F32),
            pltpu.VMEM((NC, 1, 128), F32),
            pltpu.SemaphoreType.DMA((8,)),
            pltpu.SemaphoreType.DMA((12,)),
        ],
        compiler_params=pltpu.CompilerParams(
            collective_id=0, has_side_effects=True, vmem_limit_bytes=40 * 2**20
        ),
    )(*args)
    return pl.pallas_call(
        finish,
        out_shape=(
            jax.ShapeDtypeStruct((NB, SB), BF),
            jax.ShapeDtypeStruct((SB, QB), BF),
            jax.ShapeDtypeStruct((72,), F32),
        ),
        in_specs=[vmem] * 3,
        out_specs=(anywhere, anywhere, pl.BlockSpec()),
        scratch_shapes=[pltpu.SemaphoreType.DMA((5,))],
        compiler_params=pltpu.CompilerParams(vmem_limit_bytes=2**20),
    )(pa, tu, eps)


def solution(mesh):
    placed = (
        P("row", "col"),
        P("col", None),
        P("col", "row"),
        P("row", "col"),
        P("row", "col"),
        P(),
        P(),
        P(None, "col"),
    )
    return jax.shard_map(
        per_device,
        mesh=mesh,
        in_specs=placed,
        out_specs=(P(None, "row"), P("row", "col"), P(("row", "col"))),
        check_vma=False,
    )
```

```python
import functools
import math

import jax
import jax.numpy as jnp
from jax import lax
from jax.experimental import pallas as pl
from jax.experimental.pallas import tpu as pltpu
from jax.sharding import PartitionSpec as P

NB = 128
S = 18432
NR = 16
NC = 32
SB = 1152
QB = 640
HALF = 640
MESH = pl.DeviceIdType.MESH
COL_ORDER = [z * 4 + q for z in (4, 7, 3, 5, 6, 2, 1, 0) for q in range(4) if z + q > 0]
ROW_ORDER = [y * 4 + x for y in (2, 3, 1, 0) for x in (2, 3, 1, 0) if y + x > 0]
BF = jnp.bfloat16
F32 = jnp.float32


def kernel(
    pf_hbm, dinv_hbm, rhs_hbm, trail_hbm, ff_hbm, piv_hbm, ph_hbm, th_hbm,
    pa_out, tu_out, eps_out,
    pf_v, raw, trail_v, ff_v, th_v, piv_s, ph_s,
    stage, a_land, b_land, pa, corr, c_send, c_land, hot, u_x, g_send, d_land, h_lo, h_hi, e_send, e_land,
    loc, sems,
):
    row = lax.axis_index("row")
    col = lax.axis_index("col")
    core = col % 2

    copies = [
        pltpu.make_async_copy(rhs_hbm, raw.at[:, pl.ds(0, SB)], loc.at[0]),
        pltpu.make_async_copy(dinv_hbm, raw.at[:, pl.ds(SB, NB)], loc.at[1]),
        pltpu.make_async_copy(pf_hbm, pf_v, loc.at[2]),
        pltpu.make_async_copy(th_hbm, th_v, loc.at[3]),
        pltpu.make_async_copy(piv_hbm, piv_s, loc.at[4]),
        pltpu.make_async_copy(ph_hbm, ph_s, loc.at[5]),
        pltpu.make_async_copy(ff_hbm, ff_v, loc.at[6]),
        pltpu.make_async_copy(trail_hbm, trail_v, loc.at[7]),
    ]
    for c in copies[:2]:
        c.start()

    barrier = pltpu.get_barrier_semaphore()
    for k in COL_ORDER:
        pl.semaphore_signal(barrier, inc=1, device_id=(row, col ^ k), device_id_type=MESH)
    for k in ROW_ORDER:
        pl.semaphore_signal(barrier, inc=1, device_id=(row ^ k, col), device_id_type=MESH)
    for c in copies[2:]:
        c.start()

    copies[0].wait()
    copies[1].wait()
    mine = raw[...].astype(F32)
    inverse = mine[:, SB:]
    for h in range(2):
        at = h * (SB - HALF)
        stage[h] = jnp.concatenate(
            [mine[:, at : at + 384], jnp.concatenate([mine[:, at + 384 : at + HALF], inverse], axis=1)], axis=0
        ).astype(BF)
    pl.semaphore_wait(barrier, NC - 1 + NR - 1)

    def col_copy(src, dst, target, k):
        return pltpu.make_async_remote_copy(
            src_ref=src, dst_ref=dst, send_sem=sems.at[2 * k], recv_sem=sems.at[2 * k + 1],
            device_id=(row, target), device_id_type=MESH,
        )

    def row_copy(src, dst, target, k):
        return pltpu.make_async_remote_copy(
            src_ref=src, dst_ref=dst, send_sem=sems.at[2 * k], recv_sem=sems.at[2 * k + 1],
            device_id=(target, col), device_id_type=MESH,
        )

    for k in COL_ORDER:
        target = col ^ k
        col_copy(stage.at[target % 2], a_land.at[col], target, 0).start()
    copies[2].wait()
    for k in ROW_ORDER:
        row_copy(pf_v, b_land.at[row], row ^ k, 1).start()

    a_land[col] = stage[core]
    b_land[row] = pf_v[...]
    c_land[row] = jnp.zeros((8, QB), BF)

    for c in copies[3:6]:
        c.wait()
    hx_q = th_v[pl.ds(0, 1), :]
    hy_q = th_v[pl.ds(1, 1), :]
    u_x[...] = (lax.broadcasted_iota(jnp.int32, (192, QB), 0) + hx_q - 90).astype(BF)
    hy_c = jnp.transpose(jnp.broadcast_to(hy_q.astype(F32), (128, QB)))
    hy_c = jnp.concatenate([hy_c, hy_c], axis=1).astype(jnp.int32)
    u_y = (lax.broadcasted_iota(jnp.int32, (QB, 256), 1) + hy_c - 90).astype(BF)
    hx_a = []
    for j in range(8):
        unpivoted = piv_s[row * 8 + j]
        hx_a.append(ph_s[0, unpivoted].astype(F32).astype(BF))
        hy = ph_s[1, unpivoted].astype(F32).astype(BF)
        hot[pl.ds(j * QB, QB), :] = jnp.where(u_y == hy, jnp.ones((), BF), jnp.zeros((), BF))

    col_copy(a_land.at[pl.ds(0, NC - 1)], a_land.at[pl.ds(0, NC - 1)], col ^ 1, 0).wait_recv()
    both = a_land[...].astype(F32).reshape(2 * NB, 384)
    odd = lax.broadcasted_iota(jnp.int32, (2 * NB, NB), 0) % 8 >= 4
    inverse = jnp.where(odd, both[:, 256:], 0.0)
    both = both.astype(BF)
    contract = (((0,), (0,)), ((), ()))
    mine = jnp.concatenate(
        [
            lax.dot_general(
                jnp.roll(inverse, -4, axis=0).astype(BF), both, contract, preferred_element_type=F32
            ),
            lax.dot_general(inverse.astype(BF), both[:, :256], contract, preferred_element_type=F32),
        ],
        axis=1,
    ).astype(BF)
    pa[:, pl.ds(pl.multiple_of(core * (SB - HALF), 128), HALF)] = mine
    part = pa.at[:, pl.ds(pl.multiple_of(core * HALF, 128), SB - HALF)]
    swap = col_copy(part, part, col ^ 1, 2)
    swap.start()
    copies[6].wait()
    own_rows = pl.ds(pl.multiple_of(core * (SB - HALF), 128), HALF)
    corr[...] = jnp.dot(mine, ff_v[own_rows, :], preferred_element_type=F32)
    swap.wait()

    other = pl.ds(pl.multiple_of((1 - core) * HALF, 128), SB - HALF)
    corr[...] += jnp.dot(pa[:, other], ff_v[other, :], preferred_element_type=F32)
    c_send[...] = corr[...].reshape(NR, 8, QB).astype(BF)

    for k in ROW_ORDER:
        target = row ^ k
        row_copy(c_send.at[target], c_land.at[row], target, 3).start()

    row_copy(b_land.at[pl.ds(0, NR - 1)], b_land.at[pl.ds(0, NR - 1)], row ^ 1, 1).wait_recv()
    factor = b_land[...].astype(F32).reshape(NB, QB).astype(BF)
    copies[7].wait()
    for t in range(3):
        at = pl.ds(t * 384, 384)
        update = lax.dot_general(
            pa[:, at], factor, (((0,), (0,)), ((), ())), preferred_element_type=F32
        )
        tu_out[at, :] = (trail_v[at, :].astype(F32) - update).astype(BF)
    pa_out[...] = pa[...]

    row_copy(c_land.at[pl.ds(0, NR - 1)], c_land.at[pl.ds(0, NR - 1)], row ^ 1, 3).wait_recv()
    total = corr[pl.ds(pl.multiple_of(row * 8, 8), 8), :]
    for r in range(NR):
        total = total + c_land[r].astype(F32)
    high = total.astype(BF)
    low = (total - high.astype(F32)).astype(BF)
    grid = jnp.zeros((384, 256), F32)
    for s in range(2):
        pieces = []
        for j in range(4 * s, 4 * s + 4):
            at_x = u_x[...] == hx_a[j]
            pieces.append(
                jnp.concatenate(
                    [
                        jnp.where(at_x, high[j : j + 1, :], jnp.zeros((), BF)),
                        jnp.where(at_x, low[j : j + 1, :], jnp.zeros((), BF)),
                    ],
                    axis=0,
                )
            )
        grid = grid + jnp.dot(
            jnp.concatenate(pieces, axis=1), hot[pl.ds(s * 4 * QB, 4 * QB), :], preferred_element_type=F32
        )
    grid = grid[:192] + grid[192:]
    for r in range(NR):
        g_send[r] = jnp.concatenate([grid[12 * r : 12 * r + 12], jnp.zeros((4, 256), F32)], axis=0).astype(BF)

    for k in ROW_ORDER:
        target = row ^ k
        row_copy(g_send.at[target], d_land.at[row], target, 4).start()

    d_land[row] = g_send[row]
    row_copy(d_land.at[pl.ds(0, NR - 1)], d_land.at[pl.ds(0, NR - 1)], row ^ 1, 4).wait_recv()
    summed = d_land[0].astype(F32)
    for r in range(1, NR):
        summed = summed + d_land[r].astype(F32)
    h_lo[...] = summed[:, :128]
    h_hi[...] = summed[:, 128:]

    flat = jnp.concatenate(
        [piece for t in range(3) for piece in (h_lo[pl.ds(t, 4, 3), :], h_hi[pl.ds(t, 4, 3), :][:, :64])], axis=1
    )
    for h in range(8):
        piece = jnp.concatenate([flat[:, 72 * h : 72 * h + 72], jnp.zeros((4, 56), F32)], axis=1)
        for g in range(4):
            e_send[8 * g + h] = piece[g : g + 1]

    for k in COL_ORDER:
        target = col ^ k
        col_copy(e_send.at[target], e_land.at[col], target, 5).start()

    e_land[col] = e_send[col]
    col_copy(e_land.at[pl.ds(0, NC - 1)], e_land.at[pl.ds(0, NC - 1)], col ^ 1, 5).wait_recv()
    eps_out[...] = jnp.sum(e_land[...], axis=0) * F32(1.0 / math.sqrt(S * NB))

    col_copy(a_land.at[pl.ds(0, NC - 1)], a_land.at[pl.ds(0, NC - 1)], col ^ 1, 0).wait_send()
    row_copy(b_land.at[pl.ds(0, NR - 1)], b_land.at[pl.ds(0, NR - 1)], row ^ 1, 1).wait_send()
    row_copy(c_land.at[pl.ds(0, NR - 1)], c_land.at[pl.ds(0, NR - 1)], row ^ 1, 3).wait_send()
    row_copy(d_land.at[pl.ds(0, NR - 1)], d_land.at[pl.ds(0, NR - 1)], row ^ 1, 4).wait_send()
    col_copy(e_land.at[pl.ds(0, NC - 1)], e_land.at[pl.ds(0, NC - 1)], col ^ 1, 5).wait_send()


def finish(pa_in, tu_in, eps_in, pa_out, tu_out, eps_out, eps_v, sems):
    eps_v[...] = eps_in[0, :72]
    copies = [
        pltpu.make_async_copy(tu_in.at[pl.ds(k * 288, 288)], tu_out.at[pl.ds(k * 288, 288)], sems.at[k])
        for k in range(4)
    ]
    copies.append(pltpu.make_async_copy(pa_in, pa_out, sems.at[4]))
    copies.append(pltpu.make_async_copy(eps_v, eps_out, sems.at[5]))
    for c in copies:
        c.start()
    for c in copies:
        c.wait()


def per_device(*args):
    anywhere = pl.BlockSpec(memory_space=pltpu.HBM)
    vmem = pl.BlockSpec(memory_space=pltpu.VMEM)
    args = [pltpu.with_memory_space_constraint(a, pltpu.HBM) for a in args]
    pa, tu, eps = pl.pallas_call(
        kernel,
        out_shape=(
            jax.ShapeDtypeStruct((NB, SB), BF),
            jax.ShapeDtypeStruct((SB, QB), BF),
            jax.ShapeDtypeStruct((1, 128), F32),
        ),
        in_specs=[anywhere] * 8,
        out_specs=(vmem, vmem, vmem),
        scratch_shapes=[
            pltpu.VMEM((8, QB), BF),
            pltpu.VMEM((4, SB + NB), BF),
            pltpu.VMEM((SB, QB), BF),
            pltpu.VMEM((SB, QB), BF),
            pltpu.VMEM((2, QB), jnp.int32),
            pltpu.SMEM((NB,), jnp.int32),
            pltpu.SMEM((2, NB), jnp.int32),
            pltpu.VMEM((2, 8, 384), BF),
            pltpu.VMEM((NC, 8, 384), BF),
            pltpu.VMEM((NR, 8, QB), BF),
            pltpu.VMEM((NB, SB), BF),
            pltpu.VMEM((NB, QB), F32),
            pltpu.VMEM((NR, 8, QB), BF),
            pltpu.VMEM((NR, 8, QB), BF),
            pltpu.VMEM((8 * QB, 256), BF),
            pltpu.VMEM((192, QB), BF),
            pltpu.VMEM((NR, 16, 256), BF),
            pltpu.VMEM((NR, 16, 256), BF),
            pltpu.VMEM((16, 128), F32),
            pltpu.VMEM((16, 128), F32),
            pltpu.VMEM((NC, 1, 128), F32),
            pltpu.VMEM((NC, 1, 128), F32),
            pltpu.SemaphoreType.DMA((8,)),
            pltpu.SemaphoreType.DMA((12,)),
        ],
        compiler_params=pltpu.CompilerParams(
            collective_id=0, has_side_effects=True, vmem_limit_bytes=40 * 2**20
        ),
    )(*args)
    return pl.pallas_call(
        finish,
        out_shape=(
            jax.ShapeDtypeStruct((NB, SB), BF),
            jax.ShapeDtypeStruct((SB, QB), BF),
            jax.ShapeDtypeStruct((72,), F32),
        ),
        in_specs=[vmem] * 3,
        out_specs=(anywhere,) * 3,
        scratch_shapes=[pltpu.VMEM((72,), F32), pltpu.SemaphoreType.DMA((6,))],
        compiler_params=pltpu.CompilerParams(vmem_limit_bytes=2**20),
    )(pa, tu, eps)


def solution(mesh):
    placed = (
        P("row", "col"),
        P("col", None),
        P("col", "row"),
        P("row", "col"),
        P("row", "col"),
        P(),
        P(),
        P(None, "col"),
    )
    return jax.shard_map(
        per_device,
        mesh=mesh,
        in_specs=placed,
        out_specs=(P(None, "row"), P("row", "col"), P(("row", "col"))),
        check_vma=False,
    )
```

```python
import functools
import math

import jax
import jax.numpy as jnp
from jax import lax
from jax.experimental import pallas as pl
from jax.experimental.pallas import tpu as pltpu
from jax.sharding import PartitionSpec as P

NB = 128
S = 18432
NR = 16
NC = 32
SB = 1152
QB = 640
HALF = 640
MESH = pl.DeviceIdType.MESH
COL_ORDER = [z * 4 + q for z in (4, 7, 3, 5, 6, 2, 1, 0) for q in range(4) if z + q > 0]
ROW_ORDER = [y * 4 + x for y in (2, 3, 1, 0) for x in (2, 3, 1, 0) if y + x > 0]
BF = jnp.bfloat16
F32 = jnp.float32


def kernel(
    pf_hbm, dinv_hbm, rhs_hbm, trail_hbm, ff_hbm, piv_hbm, ph_hbm, th_hbm,
    pa_out, tu_out, eps_out,
    pf_v, raw, trail_v, ff_v, th_v, piv_s, ph_s,
    stage, a_land, b_land, pa, corr, c_send, c_land, hot, u_x, g_send, d_land, h_lo, h_hi, e_send, e_land,
    loc, sems,
):
    row = lax.axis_index("row")
    col = lax.axis_index("col")
    core = col % 2
    chip = col // 2

    copies = [
        pltpu.make_async_copy(rhs_hbm, raw.at[:, pl.ds(0, SB)], loc.at[0]),
        pltpu.make_async_copy(dinv_hbm, raw.at[:, pl.ds(SB, NB)], loc.at[1]),
        pltpu.make_async_copy(pf_hbm, pf_v, loc.at[2]),
        pltpu.make_async_copy(th_hbm, th_v, loc.at[3]),
        pltpu.make_async_copy(piv_hbm, piv_s, loc.at[4]),
        pltpu.make_async_copy(ph_hbm, ph_s, loc.at[5]),
        pltpu.make_async_copy(ff_hbm, ff_v, loc.at[6]),
        pltpu.make_async_copy(trail_hbm, trail_v, loc.at[7]),
    ]
    for c in copies[:3]:
        c.start()

    barrier = pltpu.get_barrier_semaphore()
    for k in COL_ORDER:
        pl.semaphore_signal(barrier, inc=1, device_id=(row, col ^ k), device_id_type=MESH)
    for k in ROW_ORDER:
        pl.semaphore_signal(barrier, inc=1, device_id=(row ^ k, col), device_id_type=MESH)

    copies[0].wait()
    copies[1].wait()
    mine = raw[...].astype(F32)
    own = jnp.concatenate([mine[:, :HALF], mine[:, HALF:]], axis=0).astype(BF)
    stage[...] = own

    pl.semaphore_wait(barrier, NC - 1 + NR - 1)

    def col_copy(src, dst, target, k):
        return pltpu.make_async_remote_copy(
            src_ref=src, dst_ref=dst, send_sem=sems.at[2 * k], recv_sem=sems.at[2 * k + 1],
            device_id=(row, target), device_id_type=MESH,
        )

    def row_copy(src, dst, target, k):
        return pltpu.make_async_remote_copy(
            src_ref=src, dst_ref=dst, send_sem=sems.at[2 * k], recv_sem=sems.at[2 * k + 1],
            device_id=(target, col), device_id_type=MESH,
        )

    for k in COL_ORDER:
        if k % 2 == 0:
            col_copy(stage, a_land.at[core, chip], col ^ k, 0).start()
    for c in copies[3:]:
        c.start()
    copies[2].wait()
    for k in ROW_ORDER:
        row_copy(pf_v, b_land.at[row], row ^ k, 1).start()

    a_land[core, chip] = own
    b_land[row] = pf_v[...]
    c_land[row] = jnp.zeros((8, QB), BF)

    for c in copies[3:6]:
        c.wait()
    hx_q = th_v[pl.ds(0, 1), :]
    hy_q = th_v[pl.ds(1, 1), :]
    u_x[...] = (lax.broadcasted_iota(jnp.int32, (192, QB), 0) + hx_q - 90).astype(BF)
    hy_c = jnp.transpose(jnp.broadcast_to(hy_q.astype(F32), (128, QB)))
    hy_c = jnp.concatenate([hy_c, hy_c], axis=1).astype(jnp.int32)
    u_y = (lax.broadcasted_iota(jnp.int32, (QB, 256), 1) + hy_c - 90).astype(BF)
    hx_a = []
    for j in range(8):
        unpivoted = piv_s[row * 8 + j]
        hx_a.append(ph_s[0, unpivoted].astype(F32).astype(BF))
        hy = ph_s[1, unpivoted].astype(F32).astype(BF)
        hot[pl.ds(j * QB, QB), :] = jnp.where(u_y == hy, jnp.ones((), BF), jnp.zeros((), BF))

    col_copy(a_land.at[0, pl.ds(0, NC // 2 - 1)], a_land.at[0, pl.ds(0, NC // 2 - 1)], col ^ 1, 0).wait_recv()
    part = a_land.at[core]
    swap = col_copy(part, part, col ^ 1, 2)
    swap.start()
    odd = lax.broadcasted_iota(jnp.int32, (NB, NB), 0) % 8 >= 4
    contract = (((0,), (0,)), ((), ()))

    def terms(block):
        wide = block.astype(F32).reshape(NB, HALF)
        inverse = jnp.where(odd, wide[:, SB - HALF :], 0.0)
        wide = wide.astype(BF)
        return (
            lax.dot_general(
                jnp.roll(inverse, -4, axis=0).astype(BF), wide, contract, preferred_element_type=F32
            ),
            lax.dot_general(
                inverse.astype(BF), wide[:, : SB - HALF], contract, preferred_element_type=F32
            ),
        )

    near = terms(a_land[core])
    copies[6].wait()
    swap.wait()
    far = terms(a_land[1 - core])
    pa[:, pl.ds(0, HALF)] = (near[0] + far[0]).astype(BF)
    pa[:, pl.ds(HALF, SB - HALF)] = (near[1] + far[1]).astype(BF)
    corr[...] = jnp.dot(pa[...], ff_v[...], preferred_element_type=F32)
    c_send[...] = corr[...].reshape(NR, 8, QB).astype(BF)

    for k in ROW_ORDER:
        target = row ^ k
        row_copy(c_send.at[target], c_land.at[row], target, 3).start()

    row_copy(b_land.at[pl.ds(0, NR - 1)], b_land.at[pl.ds(0, NR - 1)], row ^ 1, 1).wait_recv()
    factor = b_land[...].astype(F32).reshape(NB, QB).astype(BF)
    copies[7].wait()
    for t in range(3):
        at = pl.ds(t * 384, 384)
        update = lax.dot_general(
            pa[:, at], factor, (((0,), (0,)), ((), ())), preferred_element_type=F32
        )
        tu_out[at, :] = (trail_v[at, :].astype(F32) - update).astype(BF)
    pa_out[...] = pa[...]

    row_copy(c_land.at[pl.ds(0, NR - 1)], c_land.at[pl.ds(0, NR - 1)], row ^ 1, 3).wait_recv()
    total = corr[pl.ds(pl.multiple_of(row * 8, 8), 8), :]
    for r in range(NR):
        total = total + c_land[r].astype(F32)
    high = total.astype(BF)
    low = (total - high.astype(F32)).astype(BF)
    grid = jnp.zeros((384, 256), F32)
    for s in range(2):
        pieces = []
        for j in range(4 * s, 4 * s + 4):
            at_x = u_x[...] == hx_a[j]
            pieces.append(
                jnp.concatenate(
                    [
                        jnp.where(at_x, high[j : j + 1, :], jnp.zeros((), BF)),
                        jnp.where(at_x, low[j : j + 1, :], jnp.zeros((), BF)),
                    ],
                    axis=0,
                )
            )
        grid = grid + jnp.dot(
            jnp.concatenate(pieces, axis=1), hot[pl.ds(s * 4 * QB, 4 * QB), :], preferred_element_type=F32
        )
    grid = grid[:192] + grid[192:]
    for r in range(NR):
        g_send[r] = jnp.concatenate([grid[12 * r : 12 * r + 12], jnp.zeros((4, 256), F32)], axis=0).astype(BF)

    for k in ROW_ORDER:
        target = row ^ k
        row_copy(g_send.at[target], d_land.at[row], target, 4).start()

    d_land[row] = g_send[row]
    row_copy(d_land.at[pl.ds(0, NR - 1)], d_land.at[pl.ds(0, NR - 1)], row ^ 1, 4).wait_recv()
    summed = d_land[0].astype(F32)
    for r in range(1, NR):
        summed = summed + d_land[r].astype(F32)
    h_lo[...] = summed[:, :128]
    h_hi[...] = summed[:, 128:]

    flat = jnp.concatenate(
        [piece for t in range(3) for piece in (h_lo[pl.ds(t, 4, 3), :], h_hi[pl.ds(t, 4, 3), :][:, :64])], axis=1
    )
    for h in range(8):
        piece = jnp.concatenate([flat[:, 72 * h : 72 * h + 72], jnp.zeros((4, 56), F32)], axis=1)
        for g in range(4):
            e_send[8 * g + h] = piece[g : g + 1]

    for k in COL_ORDER:
        target = col ^ k
        col_copy(e_send.at[target], e_land.at[col], target, 5).start()

    e_land[col] = e_send[col]
    col_copy(e_land.at[pl.ds(0, NC - 1)], e_land.at[pl.ds(0, NC - 1)], col ^ 1, 5).wait_recv()
    eps_out[...] = jnp.sum(e_land[...], axis=0) * F32(1.0 / math.sqrt(S * NB))

    col_copy(a_land.at[0, pl.ds(0, NC // 2 - 1)], a_land.at[0, pl.ds(0, NC // 2 - 1)], col ^ 1, 0).wait_send()
    row_copy(b_land.at[pl.ds(0, NR - 1)], b_land.at[pl.ds(0, NR - 1)], row ^ 1, 1).wait_send()
    row_copy(c_land.at[pl.ds(0, NR - 1)], c_land.at[pl.ds(0, NR - 1)], row ^ 1, 3).wait_send()
    row_copy(d_land.at[pl.ds(0, NR - 1)], d_land.at[pl.ds(0, NR - 1)], row ^ 1, 4).wait_send()
    col_copy(e_land.at[pl.ds(0, NC - 1)], e_land.at[pl.ds(0, NC - 1)], col ^ 1, 5).wait_send()


def finish(pa_in, tu_in, eps_in, pa_out, tu_out, eps_out, eps_v, sems):
    eps_v[...] = eps_in[0, :72]
    copies = [
        pltpu.make_async_copy(tu_in.at[pl.ds(k * 288, 288)], tu_out.at[pl.ds(k * 288, 288)], sems.at[k])
        for k in range(4)
    ]
    copies.append(pltpu.make_async_copy(pa_in, pa_out, sems.at[4]))
    copies.append(pltpu.make_async_copy(eps_v, eps_out, sems.at[5]))
    for c in copies:
        c.start()
    for c in copies:
        c.wait()


def per_device(*args):
    anywhere = pl.BlockSpec(memory_space=pltpu.HBM)
    vmem = pl.BlockSpec(memory_space=pltpu.VMEM)
    args = [pltpu.with_memory_space_constraint(a, pltpu.HBM) for a in args]
    pa, tu, eps = pl.pallas_call(
        kernel,
        out_shape=(
            jax.ShapeDtypeStruct((NB, SB), BF),
            jax.ShapeDtypeStruct((SB, QB), BF),
            jax.ShapeDtypeStruct((1, 128), F32),
        ),
        in_specs=[anywhere] * 8,
        out_specs=(vmem, vmem, vmem),
        scratch_shapes=[
            pltpu.VMEM((8, QB), BF),
            pltpu.VMEM((4, SB + NB), BF),
            pltpu.VMEM((SB, QB), BF),
            pltpu.VMEM((SB, QB), BF),
            pltpu.VMEM((2, QB), jnp.int32),
            pltpu.SMEM((NB,), jnp.int32),
            pltpu.SMEM((2, NB), jnp.int32),
            pltpu.VMEM((8, HALF), BF),
            pltpu.VMEM((2, NC // 2, 8, HALF), BF),
            pltpu.VMEM((NR, 8, QB), BF),
            pltpu.VMEM((NB, SB), BF),
            pltpu.VMEM((NB, QB), F32),
            pltpu.VMEM((NR, 8, QB), BF),
            pltpu.VMEM((NR, 8, QB), BF),
            pltpu.VMEM((8 * QB, 256), BF),
            pltpu.VMEM((192, QB), BF),
            pltpu.VMEM((NR, 16, 256), BF),
            pltpu.VMEM((NR, 16, 256), BF),
            pltpu.VMEM((16, 128), F32),
            pltpu.VMEM((16, 128), F32),
            pltpu.VMEM((NC, 1, 128), F32),
            pltpu.VMEM((NC, 1, 128), F32),
            pltpu.SemaphoreType.DMA((8,)),
            pltpu.SemaphoreType.DMA((12,)),
        ],
        compiler_params=pltpu.CompilerParams(
            collective_id=0, has_side_effects=True, vmem_limit_bytes=40 * 2**20
        ),
    )(*args)
    return pl.pallas_call(
        finish,
        out_shape=(
            jax.ShapeDtypeStruct((NB, SB), BF),
            jax.ShapeDtypeStruct((SB, QB), BF),
            jax.ShapeDtypeStruct((72,), F32),
        ),
        in_specs=[vmem] * 3,
        out_specs=(anywhere,) * 3,
        scratch_shapes=[pltpu.VMEM((72,), F32), pltpu.SemaphoreType.DMA((6,))],
        compiler_params=pltpu.CompilerParams(vmem_limit_bytes=2**20),
    )(pa, tu, eps)


def solution(mesh):
    placed = (
        P("row", "col"),
        P("col", None),
        P("col", "row"),
        P("row", "col"),
        P("row", "col"),
        P(),
        P(),
        P(None, "col"),
    )
    return jax.shard_map(
        per_device,
        mesh=mesh,
        in_specs=placed,
        out_specs=(P(None, "row"), P("row", "col"), P(("row", "col"))),
        check_vma=False,
    )
```

```python
import functools
import math

import jax
import jax.numpy as jnp
from jax import lax
from jax.experimental import pallas as pl
from jax.experimental.pallas import tpu as pltpu
from jax.sharding import PartitionSpec as P

NB = 128
S = 18432
NR = 16
NC = 32
SB = 1152
QB = 640
HALF = 640
MESH = pl.DeviceIdType.MESH
COL_ORDER = [z * 4 + q for z in (4, 7, 3, 5, 6, 2, 1, 0) for q in range(4) if z + q > 0]
ROW_ORDER = [y * 4 + x for y in (2, 3, 1, 0) for x in (2, 3, 1, 0) if y + x > 0]
BF = jnp.bfloat16
F32 = jnp.float32


def kernel(
    pf_hbm, dinv_hbm, rhs_hbm, trail_hbm, ff_hbm, piv_hbm, ph_hbm, th_hbm,
    pa_out, tu_out, eps_out,
    pf_v, raw, trail_v, ff_v, th_v, piv_s, ph_s,
    stage, a_land, b_land, pa, corr, c_send, c_land, hot, u_x, g_send, d_land, h_lo, h_hi, e_send, e_land,
    loc, sems,
):
    row = lax.axis_index("row")
    col = lax.axis_index("col")
    core = col % 2
    chip = col // 2

    copies = [
        pltpu.make_async_copy(rhs_hbm, raw.at[:, pl.ds(0, SB)], loc.at[0]),
        pltpu.make_async_copy(dinv_hbm, raw.at[:, pl.ds(SB, NB)], loc.at[1]),
        pltpu.make_async_copy(pf_hbm, pf_v, loc.at[2]),
        pltpu.make_async_copy(th_hbm, th_v, loc.at[3]),
        pltpu.make_async_copy(piv_hbm, piv_s, loc.at[4]),
        pltpu.make_async_copy(ph_hbm, ph_s, loc.at[5]),
        pltpu.make_async_copy(ff_hbm, ff_v, loc.at[6]),
        pltpu.make_async_copy(trail_hbm, trail_v, loc.at[7]),
    ]
    for c in copies[:3]:
        c.start()

    barrier = pltpu.get_barrier_semaphore()
    for k in COL_ORDER:
        pl.semaphore_signal(barrier, inc=1, device_id=(row, col ^ k), device_id_type=MESH)
    for k in ROW_ORDER:
        pl.semaphore_signal(barrier, inc=1, device_id=(row ^ k, col), device_id_type=MESH)

    copies[0].wait()
    copies[1].wait()
    mine = raw[...].astype(F32)
    own = jnp.concatenate([mine[:, :HALF], mine[:, HALF:]], axis=0).astype(BF)
    stage[...] = own

    pl.semaphore_wait(barrier, NC - 1 + NR - 1)

    def col_copy(src, dst, target, k):
        return pltpu.make_async_remote_copy(
            src_ref=src, dst_ref=dst, send_sem=sems.at[2 * k], recv_sem=sems.at[2 * k + 1],
            device_id=(row, target), device_id_type=MESH,
        )

    def row_copy(src, dst, target, k):
        return pltpu.make_async_remote_copy(
            src_ref=src, dst_ref=dst, send_sem=sems.at[2 * k], recv_sem=sems.at[2 * k + 1],
            device_id=(target, col), device_id_type=MESH,
        )

    for k in COL_ORDER:
        if k % 2 == 0:
            col_copy(stage, a_land.at[core, chip], col ^ k, 0).start()
    for c in copies[3:]:
        c.start()
    copies[2].wait()
    for k in ROW_ORDER:
        row_copy(pf_v, b_land.at[row], row ^ k, 1).start()

    a_land[core, chip] = own
    b_land[row] = pf_v[...]
    c_land[row] = jnp.zeros((8, QB), BF)

    for c in copies[3:6]:
        c.wait()
    hx_q = th_v[pl.ds(0, 1), :]
    hy_q = th_v[pl.ds(1, 1), :]
    u_x[...] = (lax.broadcasted_iota(jnp.int32, (192, QB), 0) + hx_q - 90).astype(BF)
    hy_c = jnp.transpose(jnp.broadcast_to(hy_q.astype(F32), (128, QB)))
    hy_c = jnp.concatenate([hy_c, hy_c], axis=1).astype(jnp.int32)
    u_y = (lax.broadcasted_iota(jnp.int32, (QB, 256), 1) + hy_c - 90).astype(BF)
    hx_a = []
    for j in range(8):
        unpivoted = piv_s[row * 8 + j]
        hx_a.append(ph_s[0, unpivoted].astype(F32).astype(BF))
        hy = ph_s[1, unpivoted].astype(F32).astype(BF)
        hot[pl.ds(j * QB, QB), :] = jnp.where(u_y == hy, jnp.ones((), BF), jnp.zeros((), BF))

    col_copy(a_land.at[0, pl.ds(0, NC // 2 - 1)], a_land.at[0, pl.ds(0, NC // 2 - 1)], col ^ 1, 0).wait_recv()
    part = a_land.at[core]
    swap = col_copy(part, part, col ^ 1, 2)
    swap.start()
    odd = lax.broadcasted_iota(jnp.int32, (NB, NB), 0) % 8 >= 4
    contract = (((0,), (0,)), ((), ()))

    def terms(block):
        wide = block.astype(F32).reshape(NB, HALF)
        inverse = jnp.where(odd, wide[:, SB - HALF :], 0.0)
        wide = wide.astype(BF)
        return (
            lax.dot_general(
                jnp.roll(inverse, -4, axis=0).astype(BF), wide, contract, preferred_element_type=F32
            ),
            lax.dot_general(
                inverse.astype(BF), wide[:, : SB - HALF], contract, preferred_element_type=F32
            ),
        )

    near = terms(a_land[core])
    copies[6].wait()
    swap.wait()
    far = terms(a_land[1 - core])
    pa[:, pl.ds(0, HALF)] = (near[0] + far[0]).astype(BF)
    pa[:, pl.ds(HALF, SB - HALF)] = (near[1] + far[1]).astype(BF)
    corr[...] = jnp.dot(pa[...], ff_v[...], preferred_element_type=F32)
    c_send[...] = corr[...].reshape(NR, 8, QB).astype(BF)

    for k in ROW_ORDER:
        target = row ^ k
        row_copy(c_send.at[target], c_land.at[row], target, 3).start()

    row_copy(b_land.at[pl.ds(0, NR - 1)], b_land.at[pl.ds(0, NR - 1)], row ^ 1, 1).wait_recv()
    factor = b_land[...].astype(F32).reshape(NB, QB).astype(BF)
    copies[7].wait()
    for t in range(3):
        at = pl.ds(t * 384, 384)
        update = lax.dot_general(
            pa[:, at], factor, (((0,), (0,)), ((), ())), preferred_element_type=F32
        )
        tu_out[at, :] = (trail_v[at, :].astype(F32) - update).astype(BF)
    pa_out[...] = pa[...]

    row_copy(c_land.at[pl.ds(0, NR - 1)], c_land.at[pl.ds(0, NR - 1)], row ^ 1, 3).wait_recv()
    total = corr[pl.ds(pl.multiple_of(row * 8, 8), 8), :]
    for r in range(NR):
        total = total + c_land[r].astype(F32)
    high = total.astype(BF)
    low = (total - high.astype(F32)).astype(BF)
    grid = jnp.zeros((384, 256), F32)
    for s in range(2):
        pieces = []
        for j in range(4 * s, 4 * s + 4):
            at_x = u_x[...] == hx_a[j]
            pieces.append(
                jnp.concatenate(
                    [
                        jnp.where(at_x, high[j : j + 1, :], jnp.zeros((), BF)),
                        jnp.where(at_x, low[j : j + 1, :], jnp.zeros((), BF)),
                    ],
                    axis=0,
                )
            )
        grid = grid + jnp.dot(
            jnp.concatenate(pieces, axis=1), hot[pl.ds(s * 4 * QB, 4 * QB), :], preferred_element_type=F32
        )
    grid = grid[:192] + grid[192:]
    for r in range(NR):
        block = grid[12 * r : 12 * r + 12]
        tail = jnp.concatenate([block[:6, 128:192], block[6:, 128:192]], axis=1)
        g_send[r] = jnp.concatenate([block[:, :128], tail, jnp.zeros((6, 128), F32)], axis=0).astype(BF)

    for k in ROW_ORDER:
        target = row ^ k
        row_copy(g_send.at[target], d_land.at[row], target, 4).start()

    d_land[row] = g_send[row]
    row_copy(d_land.at[pl.ds(0, NR - 1)], d_land.at[pl.ds(0, NR - 1)], row ^ 1, 4).wait_recv()
    summed = d_land[0].astype(F32)
    for r in range(1, NR):
        summed = summed + d_land[r].astype(F32)
    h_lo[...] = summed[:16]
    tail = jnp.concatenate([summed[12:18, :64], summed[12:18, 64:], jnp.zeros((4, 64), F32)], axis=0)
    h_hi[...] = jnp.concatenate([tail, jnp.zeros((16, 64), F32)], axis=1)

    flat = jnp.concatenate(
        [piece for t in range(3) for piece in (h_lo[pl.ds(t, 4, 3), :], h_hi[pl.ds(t, 4, 3), :][:, :64])], axis=1
    )
    for h in range(8):
        piece = jnp.concatenate([flat[:, 72 * h : 72 * h + 72], jnp.zeros((4, 56), F32)], axis=1)
        for g in range(4):
            e_send[8 * g + h] = piece[g : g + 1]

    for k in COL_ORDER:
        target = col ^ k
        col_copy(e_send.at[target], e_land.at[col], target, 5).start()

    e_land[col] = e_send[col]
    col_copy(e_land.at[pl.ds(0, NC - 1)], e_land.at[pl.ds(0, NC - 1)], col ^ 1, 5).wait_recv()
    eps_out[...] = jnp.sum(e_land[...], axis=0) * F32(1.0 / math.sqrt(S * NB))

    col_copy(a_land.at[0, pl.ds(0, NC // 2 - 1)], a_land.at[0, pl.ds(0, NC // 2 - 1)], col ^ 1, 0).wait_send()
    row_copy(b_land.at[pl.ds(0, NR - 1)], b_land.at[pl.ds(0, NR - 1)], row ^ 1, 1).wait_send()
    row_copy(c_land.at[pl.ds(0, NR - 1)], c_land.at[pl.ds(0, NR - 1)], row ^ 1, 3).wait_send()
    row_copy(d_land.at[pl.ds(0, NR - 1)], d_land.at[pl.ds(0, NR - 1)], row ^ 1, 4).wait_send()
    col_copy(e_land.at[pl.ds(0, NC - 1)], e_land.at[pl.ds(0, NC - 1)], col ^ 1, 5).wait_send()


def finish(pa_in, tu_in, eps_in, pa_out, tu_out, eps_out, eps_v, sems):
    eps_v[...] = eps_in[0, :72]
    copies = [
        pltpu.make_async_copy(tu_in.at[pl.ds(k * 288, 288)], tu_out.at[pl.ds(k * 288, 288)], sems.at[k])
        for k in range(4)
    ]
    copies.append(pltpu.make_async_copy(pa_in, pa_out, sems.at[4]))
    copies.append(pltpu.make_async_copy(eps_v, eps_out, sems.at[5]))
    for c in copies:
        c.start()
    for c in copies:
        c.wait()


def per_device(*args):
    anywhere = pl.BlockSpec(memory_space=pltpu.HBM)
    vmem = pl.BlockSpec(memory_space=pltpu.VMEM)
    args = [pltpu.with_memory_space_constraint(a, pltpu.HBM) for a in args]
    pa, tu, eps = pl.pallas_call(
        kernel,
        out_shape=(
            jax.ShapeDtypeStruct((NB, SB), BF),
            jax.ShapeDtypeStruct((SB, QB), BF),
            jax.ShapeDtypeStruct((1, 128), F32),
        ),
        in_specs=[anywhere] * 8,
        out_specs=(vmem, vmem, vmem),
        scratch_shapes=[
            pltpu.VMEM((8, QB), BF),
            pltpu.VMEM((4, SB + NB), BF),
            pltpu.VMEM((SB, QB), BF),
            pltpu.VMEM((SB, QB), BF),
            pltpu.VMEM((2, QB), jnp.int32),
            pltpu.SMEM((NB,), jnp.int32),
            pltpu.SMEM((2, NB), jnp.int32),
            pltpu.VMEM((8, HALF), BF),
            pltpu.VMEM((2, NC // 2, 8, HALF), BF),
            pltpu.VMEM((NR, 8, QB), BF),
            pltpu.VMEM((NB, SB), BF),
            pltpu.VMEM((NB, QB), F32),
            pltpu.VMEM((NR, 8, QB), BF),
            pltpu.VMEM((NR, 8, QB), BF),
            pltpu.VMEM((8 * QB, 256), BF),
            pltpu.VMEM((192, QB), BF),
            pltpu.VMEM((NR, 24, 128), BF),
            pltpu.VMEM((NR, 24, 128), BF),
            pltpu.VMEM((16, 128), F32),
            pltpu.VMEM((16, 128), F32),
            pltpu.VMEM((NC, 1, 128), F32),
            pltpu.VMEM((NC, 1, 128), F32),
            pltpu.SemaphoreType.DMA((8,)),
            pltpu.SemaphoreType.DMA((12,)),
        ],
        compiler_params=pltpu.CompilerParams(
            collective_id=0, has_side_effects=True, vmem_limit_bytes=40 * 2**20
        ),
    )(*args)
    return pl.pallas_call(
        finish,
        out_shape=(
            jax.ShapeDtypeStruct((NB, SB), BF),
            jax.ShapeDtypeStruct((SB, QB), BF),
            jax.ShapeDtypeStruct((72,), F32),
        ),
        in_specs=[vmem] * 3,
        out_specs=(anywhere,) * 3,
        scratch_shapes=[pltpu.VMEM((72,), F32), pltpu.SemaphoreType.DMA((6,))],
        compiler_params=pltpu.CompilerParams(vmem_limit_bytes=2**20),
    )(pa, tu, eps)


def solution(mesh):
    placed = (
        P("row", "col"),
        P("col", None),
        P("col", "row"),
        P("row", "col"),
        P("row", "col"),
        P(),
        P(),
        P(None, "col"),
    )
    return jax.shard_map(
        per_device,
        mesh=mesh,
        in_specs=placed,
        out_specs=(P(None, "row"), P("row", "col"), P(("row", "col"))),
        check_vma=False,
    )
```
